32 devices in a mesh: groups: 2 (over x), dp: 2 (over core), tensor: 8 (over z, y).
Axes of the slice: x: 2, y: 2, z: 4, core: 2. Of those that a mesh axis runs over, the one named last changes fastest.
Arguments:
- expert_hidden: bfloat16 [512, 8192], P(('groups', 'dp'), 'tensor'), parts along dimension 0, may hold values from -6 to 6
- expert_gain: float32 [8192], replicated, may hold values from 0.5 to 1.5
- expert_output_weight: bfloat16 [8192, 16384], P('dp', 'tensor'), may hold values from -0.0625 to 0.0625
- small_hidden: bfloat16 [2, 512, 4096], P(None, ('groups', 'dp'), 'tensor'), parts along dimension 1, may hold values from -100 to 100
- minor_norm_gains: float32 [2, 4096], P(None, 'tensor'), may hold values from 0.5 to 1.5
- minor_output_weights: bfloat16 [2, 4096, 16384], P(None, 'tensor', 'dp'), may hold values from -0.125 to 0.125
Outputs:
- steered_logits: float32 [512, 16384], P(('groups', 'dp'), 'tensor'), parts along dimension 0
The draws below stay inside these ranges and needn't reach their ends.
There are 2 independent parts, one for each index of `groups`. The reference program is written for one: setup_inputs(seed, part) draws one part's arguments, and reference() takes and returns one part's arrays. A program takes and returns all parts, laid end to end along the dimension named above; an argument that names none is the same for every part. Nothing has to cross between parts.
All inputs are finite; a program needn't handle non-finite values.
Results may differ from the reference program's by a relative error of at most 0.0029.
Values may be sent and summed in bfloat16 or wider, within the bound.
A program may use at most 256 MiB of HBM per device.

```python
import math
import jax
import jax.numpy as jnp
from jax import lax

D = 8192
DS = 4096
VOCAB = 16384
ROWS = 256


def draw_small_hidden(key, part):
    key = jax.random.fold_in(key, 11)
    first, second, third = jax.random.split(key, 3)
    positions = jnp.arange(DS, dtype=jnp.float32) / DS
    feature_scale = jnp.exp(math.log(10.0) * positions)[None, None, :] * jax.random.uniform(second, (2, 1, DS), jnp.float32, 0.5, 1.5)
    row_scale = jnp.exp(math.log(10.0) * jax.random.uniform(third, (2, ROWS, 1), jnp.float32))
    base = jnp.clip(jax.random.normal(first, (2, ROWS, DS), jnp.float32), -6.0, 6.0)
    return (base * feature_scale * row_scale * 0.1).astype(jnp.bfloat16)


def spiked(values, key, source, target, shards_of, factor):
    owner, partner = [(jnp.arange(values.shape[axis_at]) // (values.shape[axis_at] // shards_of)).reshape([-1 if axis == axis_at else 1 for axis in range(values.ndim)]) for axis_at in (source, target)]
    chosen = jax.random.permutation(key, shards_of)[partner]
    strong = (owner == chosen) | (owner == (partner + shards_of // 2) % shards_of)
    return jnp.where(strong, factor * values, values)


def level_of(stream_key, extent, pieces, smallest, high):
    def one(position, shards_of):
        heights = jax.random.uniform(jax.random.fold_in(jax.random.fold_in(stream_key, 6), position), (shards_of,), jnp.float32, smallest / len(pieces), high / len(pieces))
        return jnp.repeat(jnp.exp(heights), extent[position] // shards_of).reshape((-1,) + (1,) * (len(extent) - position - 1))

    loudness = one(*pieces[0])
    for cut in pieces[1:]:
        loudness = loudness * one(*cut)
    return loudness


def gaussian(key, extent, scale, limit, cuts=(), kind=jnp.bfloat16):
    values = jax.random.normal(key, extent, jnp.float32) * scale
    if len(cuts) > 0:
        values = level_of(key, extent, cuts, -0.22, 0.18) * values
    return jnp.clip(values, min=-limit, max=limit).astype(kind)


def noise_with(rng, dims, scale, limit, pieces, heavy, held_as=jnp.bfloat16):
    array = scale * jax.random.normal(rng, dims, jnp.float32)
    if pieces:
        array = array * level_of(rng, dims, pieces, -0.22, 0.18)
    return jnp.clip(spiked(array, jax.random.fold_in(rng, 3), *heavy), -limit, limit).astype(held_as)


def setup_inputs(seed: int = 0, part: int = 0) -> dict:
    splits = jax.random.split(jax.random.key(seed), 7)
    part_splits = jax.random.split(jax.random.fold_in(splits[6], part), 7)
    expert_hidden = gaussian(part_splits[0], (ROWS, D), 1.0, 6.0, ((0, 2), (1, 8)))
    expert_gain = jnp.clip(1.0 + 0.1 * jax.random.normal(splits[1], (D,), jnp.float32), 0.5, 1.5)
    expert_output_weight = gaussian(splits[2], (D, VOCAB), D ** -0.5, 0.0625, ((0, 2), (1, 8)))
    small_hidden = draw_small_hidden(jax.random.fold_in(jax.random.fold_in(splits[6], part), 71), part)
    minor_norm_gains = jnp.clip(1.0 + 0.1 * jax.random.normal(splits[4], (2, DS), jnp.float32), 0.5, 1.5)
    minor_output_weights = noise_with(splits[5], (2, DS, VOCAB), DS ** -0.5, 0.125, ((1, 8), (2, 2)), (1, 2, 8, 2.0))
    return {"expert_hidden": expert_hidden, "expert_gain": expert_gain, "expert_output_weight": expert_output_weight, "small_hidden": small_hidden, "minor_norm_gains": minor_norm_gains, "minor_output_weights": minor_output_weights}


def normed_rows(values, gain):
    mean_sq = lax.optimization_barrier(jnp.mean(values * values, axis=-1, keepdims=True))
    return (values * lax.rsqrt(mean_sq + 1e-05) * gain).astype(jnp.bfloat16)

def reference(expert_hidden, expert_gain, expert_output_weight, small_hidden, minor_norm_gains, minor_output_weights):
    expert_normed = normed_rows(expert_hidden.astype(jnp.float32), expert_gain)
    expert_logits = jnp.dot(expert_normed, expert_output_weight, preferred_element_type=jnp.float32)
    minor_normed_hidden = normed_rows(small_hidden.astype(jnp.float32), minor_norm_gains[:, None, :])
    minor_model_logits = jnp.einsum('dpg,dgz->dpz', minor_normed_hidden.astype(jnp.float32), minor_output_weights.astype(jnp.float32))
    return expert_logits + (minor_model_logits[0] - minor_model_logits[1])
```

```python
import functools

import jax
import jax.numpy as jnp
from jax import lax
from jax.experimental import pallas as pl
from jax.experimental.pallas import tpu as pltpu
from jax.sharding import PartitionSpec as P

F32 = jnp.float32
BF16 = jnp.bfloat16
EPS = 1e-05


def kernel(
    T, D, DS, ns,
    xe_ref, gain_ref, xs_ref, sgain_ref, we_hbm, ws_hbm, out_ref,
    we_v, ws_v, xe_n, act_e, act_s, stat_out, stat_in, ysend, yrecv, own, zsend, zrecv, epart, erecv,
    we_sem, ws_sem, st_s, st_r, as_s, as_r, eA_s, eA_r, eC_s, eC_r, y_s, y_r, z_s, z_r, ep_s, ep_r,
):
    Z = T // 2
    h = Z // 2
    R, De = xe_n.shape
    Ds = xs_ref.shape[2]
    Vt = out_ref.shape[1]
    sub = Vt // ns
    col = min(512, sub)
    c = lax.axis_index("dp")
    t = lax.axis_index("tensor")
    z = t // 2
    y = t % 2
    oc = 1 - c
    oy = 1 - y
    lo = c * h
    below = z < lo + h // 2
    cz = z // h
    zk = z % h

    def dev(cc, yy, zz):
        return {"dp": cc, "tensor": zz * 2 + yy}

    def rcopy(src, dst, s, r, d):
        return pltpu.make_async_remote_copy(
            src_ref=src, dst_ref=dst, send_sem=s, recv_sem=r, device_id=d,
            device_id_type=pl.DeviceIdType.MESH,
        )

    def arrived(ref, sem):
        pltpu.make_async_copy(ref, ref, sem).wait()

    far = [jnp.where(below, h - 1 - i, i) for i in range(h)]
    near = [jnp.where(below, i, h - 1 - i) for i in range(h)]

    def ws_copy(chunk):
        return pltpu.make_async_copy(
            ws_hbm.at[:, pl.ds(pl.multiple_of(chunk * Vt, Vt), Vt)], ws_v.at[chunk], ws_sem.at[chunk]
        )

    we_copy = pltpu.make_async_copy(we_hbm, we_v, we_sem)
    for yy in (oy, y):
        for k in far:
            ws_copy(k * 2 + yy).start()
    we_copy.start()

    barrier = pltpu.get_barrier_semaphore()

    @pl.loop(1, 2 * T)
    def _(i):
        other = lax.rem(c * T + t + i, 2 * T)
        pl.semaphore_signal(
            barrier, inc=1, device_id={"dp": other // T, "tensor": lax.rem(other, T)},
            device_id_type=pl.DeviceIdType.MESH,
        )

    xe = xe_ref[...].astype(F32)
    x0 = xs_ref[0].astype(F32)
    x1 = xs_ref[1].astype(F32)
    lane = lax.broadcasted_iota(jnp.int32, (R, 128), 1)
    se = jnp.sum(xe * xe, axis=-1, keepdims=True)
    s0 = jnp.sum(x0 * x0, axis=-1, keepdims=True)
    s1 = jnp.sum(x1 * x1, axis=-1, keepdims=True)
    packed = jnp.where(lane == 0, se, jnp.where(lane == 1, s0, jnp.where(lane == 2, s1, 0.0)))
    stat_out[...] = packed.T[0:8, :]

    pl.semaphore_wait(barrier, 2 * T - 1)

    def stat_copy(i):
        o = lax.rem(t + i, T)
        return rcopy(
            stat_out, stat_in.at[t], st_s.at[i], st_r.at[t], {"dp": c, "tensor": o}
        )

    @pl.loop(1, T)
    def _(i):
        stat_copy(i).start()

    total = stat_out[...]
    for i in range(1, T):
        o = lax.rem(t + i, T)
        arrived(stat_in.at[o], st_r.at[o])
        total = total + stat_in[o]
    row = lax.broadcasted_iota(jnp.int32, (8, R), 0)
    scale = lax.rsqrt(jnp.where(row == 0, total * (1.0 / D), total * (1.0 / DS)) + EPS)
    scale = jnp.concatenate([scale, jnp.zeros((R - 8, R), F32)], axis=0).T

    act_s[c, :, 0:Ds] = (x0 * scale[:, 1:2] * sgain_ref[0]).astype(BF16)
    act_s[c, :, Ds:2 * Ds] = -((x1 * scale[:, 2:3] * sgain_ref[1]).astype(BF16))
    as_copy = rcopy(act_s.at[c], act_s.at[c], as_s, as_r, dev(oc, y, z))
    as_copy.start()

    xe_n[...] = (xe * scale[:, 0:1] * gain_ref[t]).astype(BF16)
    across = rcopy(xe_n, act_e.at[zk, y, c], eA_s.at[1], eA_r.at[y, c], dev(cz, oy, z))
    across.start()
    to_core = rcopy(xe_n, act_e.at[zk, y, c], eA_s.at[0], eA_r.at[y, c], dev(cz, y, z))

    @pl.when(cz == c)
    def _():
        pltpu.make_async_copy(xe_n, act_e.at[zk, y, c], eA_r.at[y, c]).start()

    @pl.when(cz != c)
    def _():
        to_core.start()

    def onward(k, yy, up):
        return rcopy(
            act_e.at[k, yy], act_e.at[k, yy], eC_s.at[k, yy, up], eC_r.at[k, yy],
            dev(c, y, z + 1 if up else z - 1),
        )

    @pl.when(cz == c)
    def _():
        for yy in range(2):
            for cc in range(2):
                arrived(act_e.at[zk, yy, cc], eA_r.at[yy, cc])
            for up in range(2):
                @pl.when((z < Z - 1) if up else (z > 0))
                def _():
                    onward(zk, yy, up).start()

    as_copy.wait_recv()

    def small_tile(chunk, off):
        lhs = act_s[...].reshape(2 * R, 2 * Ds)
        return jnp.dot(lhs, ws_v[chunk, :, pl.ds(off, col)], preferred_element_type=F32)

    def y_copy(i, s):
        k = far[i]
        return rcopy(ysend.at[k, s], yrecv.at[k, s], y_s.at[k, s], y_r.at[k, s], dev(c, oy, z))

    for i in range(h):
        chunk = far[i] * 2 + oy
        ws_copy(chunk).wait()
        for s in range(ns):
            for j in range(sub // col):
                ysend[far[i], s, :, j * col:(j + 1) * col] = small_tile(chunk, s * sub + j * col).astype(BF16)
            y_copy(i, s).start()

    for i in range(h):
        chunk = far[i] * 2 + y
        ws_copy(chunk).wait()
        for s in range(ns):
            for j in range(sub // col):
                own[far[i], s, :, j * col:(j + 1) * col] = small_tile(chunk, s * sub + j * col)

    for i in range(h):
        k = near[i]
        zs = lo + k

        @pl.when(zs != z)
        def _():
            for yy in range(2):
                arrived(act_e.at[k, yy], eC_r.at[k, yy])
                @pl.when((zs < z) & (z < Z - 1))
                def _():
                    onward(k, yy, 1).start()

                @pl.when((zs > z) & (z > 0))
                def _():
                    onward(k, yy, 0).start()

    def z_copy(i, s, cc):
        k = far[i]
        return rcopy(
            zsend.at[k, s, cc], zrecv.at[z, s], z_s.at[k, s, cc], z_r.at[z, s], dev(cc, y, lo + k)
        )

    def home(i, cc):
        return (lo + far[i] == z) & (c == cc)

    for i in range(h):
        k = far[i]
        for s in range(ns):
            y_copy(i, s).wait_recv()
            for cc in range(2):
                zsend[k, s, cc] = (
                    own[k, s, cc * R:(cc + 1) * R, :] + yrecv[k, s, cc * R:(cc + 1) * R, :].astype(F32)
                ).astype(BF16)

                @pl.when(home(i, cc))
                def _():
                    pltpu.make_async_copy(zsend.at[k, s, cc], zrecv.at[z, s], z_r.at[z, s]).start()

                @pl.when(jnp.logical_not(home(i, cc)))
                def _():
                    z_copy(i, s, cc).start()

    we_copy.wait()
    ecol = min(512, Vt)

    @pl.loop(0, Vt // ecol)
    def _(j):
        at = pl.ds(pl.multiple_of(j * ecol, ecol), ecol)
        acc = jnp.zeros((2 * R, ecol), F32)
        for k in range(h):
            for yy in range(2):
                b = k * 2 + yy
                acc = acc + jnp.dot(
                    act_e[k, yy].reshape(2 * R, De), we_v[b * De:(b + 1) * De, at],
                    preferred_element_type=F32,
                )
        epart[0, :, at] = acc[0:R]
        epart[1, :, at] = acc[R:2 * R]

    ep_copy = rcopy(epart.at[oc], erecv, ep_s, ep_r, dev(oc, y, z))
    ep_copy.start()

    for zz in range(Z):
        for s in range(ns):
            arrived(zrecv.at[zz, s], z_r.at[zz, s])
    ep_copy.wait_recv()
    for s in range(ns):
        at = slice(s * sub, (s + 1) * sub)
        acc = zrecv[0, s].astype(F32)
        for zz in range(1, Z):
            acc = acc + zrecv[zz, s].astype(F32)
        out_ref[:, at] = acc + (epart[c, :, at] + erecv[:, at])

    @pl.loop(1, T)
    def _(i):
        stat_copy(i).wait_send()

    as_copy.wait_send()
    across.wait_send()

    @pl.when(cz != c)
    def _():
        to_core.wait_send()

    for i in range(h):
        k = near[i]
        zs = lo + k
        for yy in range(2):
            @pl.when((zs <= z) & (z < Z - 1))
            def _():
                onward(k, yy, 1).wait_send()

            @pl.when((zs >= z) & (z > 0))
            def _():
                onward(k, yy, 0).wait_send()
    for i in range(h):
        for s in range(ns):
            y_copy(i, s).wait_send()
            for cc in range(2):
                @pl.when(jnp.logical_not(home(i, cc)))
                def _():
                    z_copy(i, s, cc).wait_send()
    ep_copy.wait_send()


def on_device(T, xe, gain, we, xs, sgain, ws):
    R, De = xe.shape
    Ds = xs.shape[2]
    Dh, Vt = we.shape
    D, DS = De * T, Ds * T
    h = T // 4
    ns = 2 if Vt >= 1024 else 1
    sub = Vt // ns
    vmem = pl.BlockSpec(memory_space=pltpu.VMEM)
    hbm = pl.BlockSpec(memory_space=pl.ANY)
    dma = pltpu.SemaphoreType.DMA
    flops = 2 * 2 * R * (Dh * Vt + 2 * Ds * Vt * (T // 2))
    return pl.pallas_call(
        functools.partial(kernel, T, D, DS, ns),
        out_shape=jax.ShapeDtypeStruct((R, Vt), F32),
        in_specs=[vmem, vmem, vmem, vmem, hbm, hbm],
        out_specs=vmem,
        scratch_shapes=[
            pltpu.VMEM((Dh, Vt), BF16),
            pltpu.VMEM((T // 2, 2 * Ds, Vt), BF16),
            pltpu.VMEM((R, De), BF16),
            pltpu.VMEM((h, 2, 2, R, De), BF16),
            pltpu.VMEM((2, R, 2 * Ds), BF16),
            pltpu.VMEM((8, R), F32),
            pltpu.VMEM((T, 8, R), F32),
            pltpu.VMEM((h, ns, 2 * R, sub), BF16),
            pltpu.VMEM((h, ns, 2 * R, sub), BF16),
            pltpu.VMEM((h, ns, 2 * R, sub), F32),
            pltpu.VMEM((h, ns, 2, R, sub), BF16),
            pltpu.VMEM((T // 2, ns, R, sub), BF16),
            pltpu.VMEM((2, R, Vt), F32),
            pltpu.VMEM((R, Vt), F32),
            dma, dma((T // 2,)),
            dma((T,)), dma((T,)),
            dma, dma,
            dma((2,)), dma((2, 2)),
            dma((h, 2, 2)), dma((h, 2)),
            dma((h, ns)), dma((h, ns)),
            dma((h, ns, 2)), dma((T // 2, ns)),
            dma, dma,
        ],
        compiler_params=pltpu.CompilerParams(
            collective_id=0, has_side_effects=True, vmem_limit_bytes=60 * 1024 * 1024
        ),
        cost_estimate=pl.CostEstimate(flops=flops, bytes_accessed=2 * 2 * Dh * Vt, transcendentals=0),
    )(
        xe, gain.reshape(T, 1, De), xs, sgain.reshape(2, 1, Ds), we, ws.reshape(2 * Ds, ws.shape[2])
    )


def solution(mesh):
    in_specs = (
        P(("groups", "dp"), "tensor"),
        P(),
        P("dp", "tensor"),
        P(None, ("groups", "dp"), "tensor"),
        P(None, "tensor"),
        P(None, "tensor", "dp"),
    )
    out_specs = P(("groups", "dp"), "tensor")
    return jax.shard_map(
        functools.partial(on_device, mesh.shape["tensor"]),
        mesh=mesh, in_specs=in_specs, out_specs=out_specs, check_vma=False,
    )
```

```python
import functools

import jax
import jax.numpy as jnp
from jax import lax
from jax.experimental import pallas as pl
from jax.experimental.pallas import tpu as pltpu
from jax.sharding import PartitionSpec as P

F32 = jnp.float32
BF16 = jnp.bfloat16
EPS = 1e-05


def kernel(
    T, D, DS, ns,
    xe_ref, gain_ref, xs_ref, sgain_ref, we_hbm, ws_hbm, out_ref,
    we_v, ws_v, xe_n, act_e, act_s, stat_out, stat_in, ysend, yrecv, own, zsend, zrecv, psend, precv, epart, erecv,
    we_sem, ws_sem, st_s, st_r, as_s, as_r, eA_s, eA_r, eC_s, eC_r, y_s, y_r, z_s, z_r, p_s, p_r, ep_s, ep_r,
):
    Z = T // 2
    h = Z // 2
    R, De = xe_n.shape
    Ds = xs_ref.shape[2]
    Vt = out_ref.shape[1]
    sub = Vt // ns
    col = min(512, sub)
    c = lax.axis_index("dp")
    t = lax.axis_index("tensor")
    z = t // 2
    y = t % 2
    oc = 1 - c
    oy = 1 - y
    lo = c * h
    below = z < lo + h // 2
    cz = z // h
    zk = z % h

    def dev(cc, yy, zz):
        return {"dp": cc, "tensor": zz * 2 + yy}

    def rcopy(src, dst, s, r, d):
        return pltpu.make_async_remote_copy(
            src_ref=src, dst_ref=dst, send_sem=s, recv_sem=r, device_id=d,
            device_id_type=pl.DeviceIdType.MESH,
        )

    def arrived(ref, sem):
        pltpu.make_async_copy(ref, ref, sem).wait()

    far = [jnp.where(below, h - 1 - i, i) for i in range(h)]
    near = [jnp.where(below, i, h - 1 - i) for i in range(h)]

    def ws_copy(chunk):
        return pltpu.make_async_copy(
            ws_hbm.at[:, pl.ds(pl.multiple_of(chunk * Vt, Vt), Vt)], ws_v.at[chunk], ws_sem.at[chunk]
        )

    we_copy = pltpu.make_async_copy(we_hbm, we_v, we_sem)
    for yy in (oy, y):
        for k in far:
            ws_copy(k * 2 + yy).start()
    we_copy.start()

    barrier = pltpu.get_barrier_semaphore()

    @pl.loop(1, 2 * T)
    def _(i):
        other = lax.rem(c * T + t + i, 2 * T)
        pl.semaphore_signal(
            barrier, inc=1, device_id={"dp": other // T, "tensor": lax.rem(other, T)},
            device_id_type=pl.DeviceIdType.MESH,
        )

    xe = xe_ref[...].astype(F32)
    x0 = xs_ref[0].astype(F32)
    x1 = xs_ref[1].astype(F32)
    lane = lax.broadcasted_iota(jnp.int32, (R, 128), 1)
    se = jnp.sum(xe * xe, axis=-1, keepdims=True)
    s0 = jnp.sum(x0 * x0, axis=-1, keepdims=True)
    s1 = jnp.sum(x1 * x1, axis=-1, keepdims=True)
    packed = jnp.where(lane == 0, se, jnp.where(lane == 1, s0, jnp.where(lane == 2, s1, 0.0)))
    stat_out[...] = packed.T[0:8, :]

    pl.semaphore_wait(barrier, 2 * T - 1)

    def stat_copy(i):
        o = lax.rem(t + i, T)
        return rcopy(
            stat_out, stat_in.at[t], st_s.at[i], st_r.at[t], {"dp": c, "tensor": o}
        )

    @pl.loop(1, T)
    def _(i):
        stat_copy(i).start()

    total = stat_out[...]
    for i in range(1, T):
        o = lax.rem(t + i, T)
        arrived(stat_in.at[o], st_r.at[o])
        total = total + stat_in[o]
    row = lax.broadcasted_iota(jnp.int32, (8, R), 0)
    scale = lax.rsqrt(jnp.where(row == 0, total * (1.0 / D), total * (1.0 / DS)) + EPS)
    scale = jnp.concatenate([scale, jnp.zeros((R - 8, R), F32)], axis=0).T

    act_s[c, :, 0:Ds] = (x0 * scale[:, 1:2] * sgain_ref[0:1, :]).astype(BF16)
    act_s[c, :, Ds:2 * Ds] = -((x1 * scale[:, 2:3] * sgain_ref[1:2, :]).astype(BF16))
    as_copy = rcopy(act_s.at[c], act_s.at[c], as_s, as_r, dev(oc, y, z))
    as_copy.start()

    xe_n[...] = (xe * scale[:, 0:1] * gain_ref[t]).astype(BF16)
    across = rcopy(xe_n, act_e.at[zk, y, c], eA_s.at[1], eA_r.at[y, c], dev(cz, oy, z))
    across.start()
    to_core = rcopy(xe_n, act_e.at[zk, y, c], eA_s.at[0], eA_r.at[y, c], dev(cz, y, z))

    @pl.when(cz == c)
    def _():
        pltpu.make_async_copy(xe_n, act_e.at[zk, y, c], eA_r.at[y, c]).start()

    @pl.when(cz != c)
    def _():
        to_core.start()

    def onward(k, yy, up):
        return rcopy(
            act_e.at[k, yy], act_e.at[k, yy], eC_s.at[k, yy, up], eC_r.at[k, yy],
            dev(c, y, z + 1 if up else z - 1),
        )

    @pl.when(cz == c)
    def _():
        for yy in range(2):
            for cc in range(2):
                arrived(act_e.at[zk, yy, cc], eA_r.at[yy, cc])
            for up in range(2):
                @pl.when((z < Z - 1) if up else (z > 0))
                def _():
                    onward(zk, yy, up).start()

    as_copy.wait_recv()

    def small_tile(chunk, off):
        lhs = act_s[...].reshape(2 * R, 2 * Ds)
        return jnp.dot(lhs, ws_v[chunk, :, pl.ds(off, col)], preferred_element_type=F32)

    def y_copy(i, s):
        k = far[i]
        return rcopy(ysend.at[k, s], yrecv.at[k, s], y_s.at[k, s], y_r.at[k, s], dev(c, oy, z))

    for i in range(h):
        chunk = far[i] * 2 + oy
        ws_copy(chunk).wait()
        for s in range(ns):
            for j in range(sub // col):
                ysend[far[i], s, :, j * col:(j + 1) * col] = small_tile(chunk, s * sub + j * col).astype(BF16)
            y_copy(i, s).start()

    for i in range(h):
        chunk = far[i] * 2 + y
        ws_copy(chunk).wait()
        for s in range(ns):
            for j in range(sub // col):
                own[far[i], s, :, j * col:(j + 1) * col] = small_tile(chunk, s * sub + j * col)

    pair = z // 2
    pairs = Z // 2
    mate = z + 1 - 2 * (z % 2)

    def hand_on(i, yy, sending):
        k = near[i]
        zs = lo + k

        @pl.when((zs < z) & (z < Z - 1))
        def _():
            if sending:
                arrived(act_e.at[k, yy], eC_r.at[k, yy])
                onward(k, yy, 1).start()
            else:
                onward(k, yy, 1).wait_send()

        @pl.when((zs > z) & (z > 0))
        def _():
            if sending:
                arrived(act_e.at[k, yy], eC_r.at[k, yy])
                onward(k, yy, 0).start()
            else:
                onward(k, yy, 0).wait_send()

    def last_stop(i, yy):
        k = near[i]
        zs = lo + k

        @pl.when(((zs < z) & (z == Z - 1)) | ((zs > z) & (z == 0)))
        def _():
            arrived(act_e.at[k, yy], eC_r.at[k, yy])

    def inside(i):
        return (lo + far[i]) // 2 == pair

    def nearer(i):
        return jnp.where(lo + far[i] > z, z % 2 == 1, z % 2 == 0)

    def home(i, cc):
        return (lo + far[i] == z) & (c == cc)

    def z_copy(i, s, cc):
        k = far[i]
        slot = jnp.where(inside(i) & (lo + k != z), pairs, pair)
        return rcopy(
            zsend.at[k, s, cc], zrecv.at[slot, s], z_s.at[k, s, cc], z_r.at[slot, s], dev(cc, y, lo + k)
        )

    def p_copy(i, s):
        k = far[i]
        return rcopy(psend.at[k, s], precv.at[k, s], p_s.at[k, s], p_r.at[k, s], dev(c, y, mate))

    def along_z(i, s):
        k = far[i]
        y_copy(i, s).wait_recv()
        leaves = jnp.logical_not(inside(i)) & jnp.logical_not(nearer(i))

        @pl.when(leaves)
        def _():
            psend[k, s] = (own[k, s] + yrecv[k, s].astype(F32)).astype(BF16)
            p_copy(i, s).start()

        @pl.when(inside(i))
        def _():
            for cc in range(2):
                at = slice(cc * R, (cc + 1) * R)
                zsend[k, s, cc] = (own[k, s, at, :] + yrecv[k, s, at, :].astype(F32)).astype(BF16)

        @pl.when(jnp.logical_not(inside(i)) & nearer(i))
        def _():
            p_copy(i, s).wait_recv()
            for cc in range(2):
                at = slice(cc * R, (cc + 1) * R)
                zsend[k, s, cc] = (
                    own[k, s, at, :] + yrecv[k, s, at, :].astype(F32) + precv[k, s, at, :].astype(F32)
                ).astype(BF16)

        for cc in range(2):
            @pl.when(home(i, cc))
            def _():
                pltpu.make_async_copy(zsend.at[k, s, cc], zrecv.at[pair, s], z_r.at[pair, s]).start()

            @pl.when(jnp.logical_not(home(i, cc)) & jnp.logical_not(leaves))
            def _():
                z_copy(i, s, cc).start()

    items = [(i, s) for i in range(h) for s in range(ns)]
    for n in range(max(h, len(items))):
        if n < h:
            for yy in range(2):
                hand_on(n, yy, True)
        if n < len(items):
            along_z(*items[n])
    for i in range(h):
        for yy in range(2):
            last_stop(i, yy)

    we_copy.wait()
    ecol = min(512, Vt)

    @pl.loop(0, Vt // ecol)
    def _(j):
        at = pl.ds(pl.multiple_of(j * ecol, ecol), ecol)
        acc = jnp.zeros((2 * R, ecol), F32)
        for k in range(h):
            for yy in range(2):
                b = k * 2 + yy
                acc = acc + jnp.dot(
                    act_e[k, yy].reshape(2 * R, De), we_v[b * De:(b + 1) * De, at],
                    preferred_element_type=F32,
                )
        epart[0, :, at] = acc[0:R]
        epart[1, :, at] = acc[R:2 * R]

    ep_copy = rcopy(epart.at[oc], erecv, ep_s, ep_r, dev(oc, y, z))
    ep_copy.start()

    for zz in range(pairs + 1):
        for s in range(ns):
            arrived(zrecv.at[zz, s], z_r.at[zz, s])
    ep_copy.wait_recv()
    for s in range(ns):
        at = slice(s * sub, (s + 1) * sub)
        acc = zrecv[0, s].astype(F32)
        for zz in range(1, pairs + 1):
            acc = acc + zrecv[zz, s].astype(F32)
        out_ref[:, at] = acc + (epart[c, :, at] + erecv[:, at])

    @pl.loop(1, T)
    def _(i):
        stat_copy(i).wait_send()

    as_copy.wait_send()
    across.wait_send()

    @pl.when(cz != c)
    def _():
        to_core.wait_send()

    @pl.when(cz == c)
    def _():
        for yy in range(2):
            for up in range(2):
                @pl.when((z < Z - 1) if up else (z > 0))
                def _():
                    onward(zk, yy, up).wait_send()

    for i in range(h):
        for yy in range(2):
            hand_on(i, yy, False)
        leaves = jnp.logical_not(inside(i)) & jnp.logical_not(nearer(i))
        for s in range(ns):
            y_copy(i, s).wait_send()

            @pl.when(leaves)
            def _():
                p_copy(i, s).wait_send()

            for cc in range(2):
                @pl.when(jnp.logical_not(home(i, cc)) & jnp.logical_not(leaves))
                def _():
                    z_copy(i, s, cc).wait_send()
    ep_copy.wait_send()


def on_device(T, xe, gain, we, xs, sgain, ws):
    R, De = xe.shape
    Ds = xs.shape[2]
    Dh, Vt = we.shape
    D, DS = De * T, Ds * T
    h = T // 4
    ns = 2 if Vt >= 1024 else 1
    sub = Vt // ns
    vmem = pl.BlockSpec(memory_space=pltpu.VMEM)
    hbm = pl.BlockSpec(memory_space=pl.ANY)
    dma = pltpu.SemaphoreType.DMA
    flops = 2 * 2 * R * (Dh * Vt + 2 * Ds * Vt * (T // 2))
    return pl.pallas_call(
        functools.partial(kernel, T, D, DS, ns),
        out_shape=jax.ShapeDtypeStruct((R, Vt), F32),
        in_specs=[vmem, vmem, vmem, vmem, hbm, hbm],
        out_specs=vmem,
        scratch_shapes=[
            pltpu.VMEM((Dh, Vt), BF16),
            pltpu.VMEM((T // 2, 2 * Ds, Vt), BF16),
            pltpu.VMEM((R, De), BF16),
            pltpu.VMEM((h, 2, 2, R, De), BF16),
            pltpu.VMEM((2, R, 2 * Ds), BF16),
            pltpu.VMEM((8, R), F32),
            pltpu.VMEM((T, 8, R), F32),
            pltpu.VMEM((h, ns, 2 * R, sub), BF16),
            pltpu.VMEM((h, ns, 2 * R, sub), BF16),
            pltpu.VMEM((h, ns, 2 * R, sub), F32),
            pltpu.VMEM((h, ns, 2, R, sub), BF16),
            pltpu.VMEM((T // 4 + 1, ns, R, sub), BF16),
            pltpu.VMEM((h, ns, 2 * R, sub), BF16),
            pltpu.VMEM((h, ns, 2 * R, sub), BF16),
            pltpu.VMEM((2, R, Vt), F32),
            pltpu.VMEM((R, Vt), F32),
            dma, dma((T // 2,)),
            dma((T,)), dma((T,)),
            dma, dma,
            dma((2,)), dma((2, 2)),
            dma((h, 2, 2)), dma((h, 2)),
            dma((h, ns)), dma((h, ns)),
            dma((h, ns, 2)), dma((T // 4 + 1, ns)),
            dma((h, ns)), dma((h, ns)),
            dma, dma,
        ],
        compiler_params=pltpu.CompilerParams(
            collective_id=0, has_side_effects=True, vmem_limit_bytes=60 * 1024 * 1024
        ),
        cost_estimate=pl.CostEstimate(flops=flops, bytes_accessed=2 * 2 * Dh * Vt, transcendentals=0),
    )(
        xe, gain.reshape(T, 1, De), xs, sgain, we, ws.reshape(2 * Ds, ws.shape[2])
    )


def solution(mesh):
    in_specs = (
        P(("groups", "dp"), "tensor"),
        P(),
        P("dp", "tensor"),
        P(None, ("groups", "dp"), "tensor"),
        P(None, "tensor"),
        P(None, "tensor", "dp"),
    )
    out_specs = P(("groups", "dp"), "tensor")
    return jax.shard_map(
        functools.partial(on_device, mesh.shape["tensor"]),
        mesh=mesh, in_specs=in_specs, out_specs=out_specs, check_vma=False,
    )
```

```python
import functools

import jax
import jax.numpy as jnp
from jax import lax
from jax.experimental import pallas as pl
from jax.experimental.pallas import tpu as pltpu
from jax.sharding import PartitionSpec as P

F32 = jnp.float32
BF16 = jnp.bfloat16
EPS = 1e-05


def kernel(
    T, D, DS, ns,
    xe_ref, gain_ref, xs_ref, sgain_ref, we_hbm, ws_hbm, out_ref,
    we_v, ws_v, act_n, scales, act_e, act_s, stat_out, stat_in, ysend, yrecv, own, zsend, zrecv, psend, precv, epart, erecv,
    we_sem, ws_sem, st_s, st_r, as_s, as_r, sc_s, sc_r, eA_s, eA_r, eC_s, eC_r, y_s, y_r, z_s, z_r, p_s, p_r, ep_s, ep_r,
):
    Z = T // 2
    h = Z // 2
    R, De = xe_ref.shape
    Ds = xs_ref.shape[2]
    Vt = out_ref.shape[1]
    sub = Vt // ns
    col = min(512, sub)
    c = lax.axis_index("dp")
    t = lax.axis_index("tensor")
    z = t // 2
    y = t % 2
    oc = 1 - c
    oy = 1 - y
    lo = c * h
    below = z < lo + h // 2
    cz = z // h
    zk = z % h

    def dev(cc, yy, zz):
        return {"dp": cc, "tensor": zz * 2 + yy}

    def rcopy(src, dst, s, r, d):
        return pltpu.make_async_remote_copy(
            src_ref=src, dst_ref=dst, send_sem=s, recv_sem=r, device_id=d,
            device_id_type=pl.DeviceIdType.MESH,
        )

    def arrived(ref, sem):
        pltpu.make_async_copy(ref, ref, sem).wait()

    far = [jnp.where(below, h - 1 - i, i) for i in range(h)]
    near = [jnp.where(below, i, h - 1 - i) for i in range(h)]

    def ws_copy(chunk):
        return pltpu.make_async_copy(
            ws_hbm.at[:, pl.ds(pl.multiple_of(chunk * Vt, Vt), Vt)], ws_v.at[chunk], ws_sem.at[chunk]
        )

    we_copy = pltpu.make_async_copy(we_hbm, we_v, we_sem)
    for yy in (oy, y):
        for k in far:
            ws_copy(k * 2 + yy).start()
    we_copy.start()

    barrier = pltpu.get_barrier_semaphore()

    @pl.loop(1, 2 * T)
    def _(i):
        other = lax.rem(c * T + t + i, 2 * T)
        pl.semaphore_signal(
            barrier, inc=1, device_id={"dp": other // T, "tensor": lax.rem(other, T)},
            device_id_type=pl.DeviceIdType.MESH,
        )

    xe = xe_ref[...].astype(F32)
    x0 = xs_ref[0].astype(F32)
    x1 = xs_ref[1].astype(F32)
    lane = lax.broadcasted_iota(jnp.int32, (R, 128), 1)
    se = jnp.sum(xe * xe, axis=-1, keepdims=True)
    s0 = jnp.sum(x0 * x0, axis=-1, keepdims=True)
    s1 = jnp.sum(x1 * x1, axis=-1, keepdims=True)
    packed = jnp.where(lane == 0, se, jnp.where(lane == 1, s0, jnp.where(lane == 2, s1, 0.0)))
    stat_out[...] = packed.T[0:8, :]

    pl.semaphore_wait(barrier, 2 * T - 1)

    def stat_copy(i):
        o = lax.rem(t + i, T)
        return rcopy(
            stat_out, stat_in.at[t], st_s.at[i], st_r.at[t], {"dp": c, "tensor": o}
        )

    @pl.loop(1, T)
    def _(i):
        stat_copy(i).start()

    to_core = rcopy(xe_ref, act_e.at[zk, y, c], eA_s.at[0], eA_r.at[y, c], dev(cz, y, z))
    across = rcopy(xe_ref, act_e.at[zk, y, c], eA_s.at[1], eA_r.at[y, c], dev(cz, oy, z))

    @pl.when(cz == c)
    def _():
        pltpu.make_async_copy(xe_ref, act_e.at[zk, y, c], eA_r.at[y, c]).start()

    @pl.when(cz != c)
    def _():
        to_core.start()

    across.start()

    def onward(k, yy, up):
        return rcopy(
            act_e.at[k, yy], act_e.at[k, yy], eC_s.at[k, yy, up], eC_r.at[k, yy],
            dev(c, y, z + 1 if up else z - 1),
        )

    def set_out(yy):
        @pl.when(cz == c)
        def _():
            for cc in range(2):
                arrived(act_e.at[zk, yy, cc], eA_r.at[yy, cc])
            for up in range(2):
                @pl.when((z < Z - 1) if up else (z > 0))
                def _():
                    onward(zk, yy, up).start()

    set_out(y)

    total = stat_out[...]
    for i in range(1, T):
        o = lax.rem(t + i, T)
        arrived(stat_in.at[o], st_r.at[o])
        total = total + stat_in[o]
    row = lax.broadcasted_iota(jnp.int32, (8, R), 0)
    scale = lax.rsqrt(jnp.where(row == 0, total * (1.0 / D), total * (1.0 / DS)) + EPS)
    scale = jnp.concatenate([scale, jnp.zeros((R - 8, R), F32)], axis=0).T

    act_s[c, :, 0:Ds] = (x0 * scale[:, 1:2] * sgain_ref[0:1, :]).astype(BF16)
    act_s[c, :, Ds:2 * Ds] = -((x1 * scale[:, 2:3] * sgain_ref[1:2, :]).astype(BF16))
    as_copy = rcopy(act_s.at[c], act_s.at[c], as_s, as_r, dev(oc, y, z))
    as_copy.start()
    scales[c] = scale
    sc_copy = rcopy(scales.at[c], scales.at[c], sc_s, sc_r, dev(oc, y, z))
    sc_copy.start()

    as_copy.wait_recv()

    def small_tile(chunk, off):
        lhs = act_s[...].reshape(2 * R, 2 * Ds)
        return jnp.dot(lhs, ws_v[chunk, :, pl.ds(off, col)], preferred_element_type=F32)

    def y_copy(i, s):
        k = far[i]
        return rcopy(ysend.at[k, s], yrecv.at[k, s], y_s.at[k, s], y_r.at[k, s], dev(c, oy, z))

    for i in range(h):
        chunk = far[i] * 2 + oy
        ws_copy(chunk).wait()
        for s in range(ns):
            for j in range(sub // col):
                ysend[far[i], s, :, j * col:(j + 1) * col] = small_tile(chunk, s * sub + j * col).astype(BF16)
            y_copy(i, s).start()
        if i == 0:
            set_out(oy)

    for i in range(h):
        chunk = far[i] * 2 + y
        ws_copy(chunk).wait()
        for s in range(ns):
            for j in range(sub // col):
                own[far[i], s, :, j * col:(j + 1) * col] = small_tile(chunk, s * sub + j * col)

    pair = z // 2
    pairs = Z // 2
    mate = z + 1 - 2 * (z % 2)

    def hand_on(i, yy, sending):
        k = near[i]
        zs = lo + k

        @pl.when((zs < z) & (z < Z - 1))
        def _():
            if sending:
                arrived(act_e.at[k, yy], eC_r.at[k, yy])
                onward(k, yy, 1).start()
            else:
                onward(k, yy, 1).wait_send()

        @pl.when((zs > z) & (z > 0))
        def _():
            if sending:
                arrived(act_e.at[k, yy], eC_r.at[k, yy])
                onward(k, yy, 0).start()
            else:
                onward(k, yy, 0).wait_send()

    def last_stop(i, yy):
        k = near[i]
        zs = lo + k

        @pl.when(((zs < z) & (z == Z - 1)) | ((zs > z) & (z == 0)))
        def _():
            arrived(act_e.at[k, yy], eC_r.at[k, yy])

    def inside(i):
        return (lo + far[i]) // 2 == pair

    def nearer(i):
        return jnp.where(lo + far[i] > z, z % 2 == 1, z % 2 == 0)

    def home(i, cc):
        return (lo + far[i] == z) & (c == cc)

    def z_copy(i, s, cc):
        k = far[i]
        slot = jnp.where(inside(i) & (lo + k != z), pairs, pair)
        return rcopy(
            zsend.at[k, s, cc], zrecv.at[slot, s], z_s.at[k, s, cc], z_r.at[slot, s], dev(cc, y, lo + k)
        )

    def p_copy(i, s):
        k = far[i]
        return rcopy(psend.at[k, s], precv.at[k, s], p_s.at[k, s], p_r.at[k, s], dev(c, y, mate))

    def along_z(i, s):
        k = far[i]
        y_copy(i, s).wait_recv()
        leaves = jnp.logical_not(inside(i)) & jnp.logical_not(nearer(i))

        @pl.when(leaves)
        def _():
            psend[k, s] = (own[k, s] + yrecv[k, s].astype(F32)).astype(BF16)
            p_copy(i, s).start()

        @pl.when(inside(i))
        def _():
            for cc in range(2):
                at = slice(cc * R, (cc + 1) * R)
                zsend[k, s, cc] = (own[k, s, at, :] + yrecv[k, s, at, :].astype(F32)).astype(BF16)

        @pl.when(jnp.logical_not(inside(i)) & nearer(i))
        def _():
            p_copy(i, s).wait_recv()
            for cc in range(2):
                at = slice(cc * R, (cc + 1) * R)
                zsend[k, s, cc] = (
                    own[k, s, at, :] + yrecv[k, s, at, :].astype(F32) + precv[k, s, at, :].astype(F32)
                ).astype(BF16)

        for cc in range(2):
            @pl.when(home(i, cc))
            def _():
                pltpu.make_async_copy(zsend.at[k, s, cc], zrecv.at[pair, s], z_r.at[pair, s]).start()

            @pl.when(jnp.logical_not(home(i, cc)) & jnp.logical_not(leaves))
            def _():
                z_copy(i, s, cc).start()

    ecol = min(512, Vt)

    def expert(i):
        k = near[i]
        for yy in range(2):
            last_stop(i, yy)
            for cc in range(2):
                rows = act_e[k, yy, cc].astype(F32)
                act_n[yy, cc * R:(cc + 1) * R, :] = (
                    rows * scales[cc, :, 0:1] * gain_ref[(lo + k) * 2 + yy]
                ).astype(BF16)

        @pl.loop(0, Vt // ecol)
        def _(j):
            at = pl.ds(pl.multiple_of(j * ecol, ecol), ecol)
            acc = jnp.zeros((2 * R, ecol), F32)
            for yy in range(2):
                depth = pl.ds(pl.multiple_of((k * 2 + yy) * De, De), De)
                acc = acc + jnp.dot(act_n[yy], we_v[depth, at], preferred_element_type=F32)
            for cc in range(2):
                part = acc[cc * R:(cc + 1) * R]
                epart[cc, :, at] = part if i == 0 else epart[cc, :, at] + part

    items = [(i, s) for i in range(h) for s in range(ns)]
    for n in range(len(items)):
        if n < h:
            for yy in (y, oy):
                hand_on(n, yy, True)
        if n == len(items) - 2:
            sc_copy.wait_recv()
            we_copy.wait()
            for i in range(h - 1):
                expert(i)
        along_z(*items[n])
    expert(h - 1)

    ep_copy = rcopy(epart.at[oc], erecv, ep_s, ep_r, dev(oc, y, z))
    ep_copy.start()

    for zz in range(pairs + 1):
        for s in range(ns):
            arrived(zrecv.at[zz, s], z_r.at[zz, s])
    ep_copy.wait_recv()
    for s in range(ns):
        at = slice(s * sub, (s + 1) * sub)
        acc = zrecv[0, s].astype(F32)
        for zz in range(1, pairs + 1):
            acc = acc + zrecv[zz, s].astype(F32)
        out_ref[:, at] = acc + (epart[c, :, at] + erecv[:, at])

    @pl.loop(1, T)
    def _(i):
        stat_copy(i).wait_send()

    as_copy.wait_send()
    sc_copy.wait_send()
    across.wait_send()

    @pl.when(cz != c)
    def _():
        to_core.wait_send()

    @pl.when(cz == c)
    def _():
        for yy in range(2):
            for up in range(2):
                @pl.when((z < Z - 1) if up else (z > 0))
                def _():
                    onward(zk, yy, up).wait_send()

    for i in range(h):
        for yy in range(2):
            hand_on(i, yy, False)
        leaves = jnp.logical_not(inside(i)) & jnp.logical_not(nearer(i))
        for s in range(ns):
            y_copy(i, s).wait_send()

            @pl.when(leaves)
            def _():
                p_copy(i, s).wait_send()

            for cc in range(2):
                @pl.when(jnp.logical_not(home(i, cc)) & jnp.logical_not(leaves))
                def _():
                    z_copy(i, s, cc).wait_send()
    ep_copy.wait_send()


def on_device(T, xe, gain, we, xs, sgain, ws):
    R, De = xe.shape
    Ds = xs.shape[2]
    Dh, Vt = we.shape
    D, DS = De * T, Ds * T
    h = T // 4
    ns = 4 if Vt >= 1024 else 1
    sub = Vt // ns
    vmem = pl.BlockSpec(memory_space=pltpu.VMEM)
    hbm = pl.BlockSpec(memory_space=pl.ANY)
    dma = pltpu.SemaphoreType.DMA
    flops = 2 * 2 * R * (Dh * Vt + 2 * Ds * Vt * (T // 2))
    return pl.pallas_call(
        functools.partial(kernel, T, D, DS, ns),
        out_shape=jax.ShapeDtypeStruct((R, Vt), F32),
        in_specs=[vmem, vmem, vmem, vmem, hbm, hbm],
        out_specs=vmem,
        scratch_shapes=[
            pltpu.VMEM((Dh, Vt), BF16),
            pltpu.VMEM((T // 2, 2 * Ds, Vt), BF16),
            pltpu.VMEM((2, 2 * R, De), BF16),
            pltpu.VMEM((2, R, R), F32),
            pltpu.VMEM((h, 2, 2, R, De), BF16),
            pltpu.VMEM((2, R, 2 * Ds), BF16),
            pltpu.VMEM((8, R), F32),
            pltpu.VMEM((T, 8, R), F32),
            pltpu.VMEM((h, ns, 2 * R, sub), BF16),
            pltpu.VMEM((h, ns, 2 * R, sub), BF16),
            pltpu.VMEM((h, ns, 2 * R, sub), F32),
            pltpu.VMEM((h, ns, 2, R, sub), BF16),
            pltpu.VMEM((T // 4 + 1, ns, R, sub), BF16),
            pltpu.VMEM((h, ns, 2 * R, sub), BF16),
            pltpu.VMEM((h, ns, 2 * R, sub), BF16),
            pltpu.VMEM((2, R, Vt), F32),
            pltpu.VMEM((R, Vt), F32),
            dma, dma((T // 2,)),
            dma((T,)), dma((T,)),
            dma, dma,
            dma, dma,
            dma((2,)), dma((2, 2)),
            dma((h, 2, 2)), dma((h, 2)),
            dma((h, ns)), dma((h, ns)),
            dma((h, ns, 2)), dma((T // 4 + 1, ns)),
            dma((h, ns)), dma((h, ns)),
            dma, dma,
        ],
        compiler_params=pltpu.CompilerParams(
            collective_id=0, has_side_effects=True, vmem_limit_bytes=60 * 1024 * 1024
        ),
        cost_estimate=pl.CostEstimate(flops=flops, bytes_accessed=2 * 2 * Dh * Vt, transcendentals=0),
    )(
        xe, gain.reshape(T, 1, De), xs, sgain, we, ws.reshape(2 * Ds, ws.shape[2])
    )


def solution(mesh):
    in_specs = (
        P(("groups", "dp"), "tensor"),
        P(),
        P("dp", "tensor"),
        P(None, ("groups", "dp"), "tensor"),
        P(None, "tensor"),
        P(None, "tensor", "dp"),
    )
    out_specs = P(("groups", "dp"), "tensor")
    return jax.shard_map(
        functools.partial(on_device, mesh.shape["tensor"]),
        mesh=mesh, in_specs=in_specs, out_specs=out_specs, check_vma=False,
    )
```
